32 devices in a mesh: lon: 8 (over y, x, core), lat: 4 (over z).
Axes of the slice: x: 2, y: 2, z: 4, core: 2. Of those that a mesh axis runs over, the one named last changes fastest.
Arguments:
- thermal_anomaly: float32 [8, 128, 1024], P(None, 'lat', 'lon'), may hold values from -6 to 6
- saltiness_anomaly: float32 [8, 128, 1024], P(None, 'lat', 'lon'), may hold values from -6 to 6
- zonal_velocity: float32 [8, 128, 1024], P(None, 'lat', 'lon'), may hold values from -3 to 3
- meridional_velocity: float32 [8, 128, 1024], P(None, 'lat', 'lon'), may hold values from -3 to 3
- sea_point_indicator: int32 [8, 128, 1024], P(None, 'lat', 'lon'), may hold values 0 or 1
Outputs:
- temperature_out: float32 [8, 128, 1024], P(None, 'lat', 'lon')
- salinity_out: float32 [8, 128, 1024], P(None, 'lat', 'lon')
- east_out: float32 [8, 128, 1024], P(None, 'lat', 'lon')
- north_out: float32 [8, 128, 1024], P(None, 'lat', 'lon')
The draws below stay inside these ranges and needn't reach their ends.
All inputs are finite; a program needn't handle non-finite values. No bound on the sum of `sea_point_indicator` on one device may be relied on, other than what follows from the above.
Results may differ from the reference program's by a relative error of at most 0.00002.
Values sent between devices are 32-bit elements; how exact they have to be, the bound alone decides.
A program may use at most 64 MiB of HBM per device.

```python
import jax
import jax.numpy as jnp

LAYER_TOTAL = 8
STEPS = 2
MERIDIAN_TOTAL = 1024
PARALLEL_TOTAL = 128


def set_ends(result, stream_key, least, high):
    spot = [jax.random.randint(jax.random.fold_in(stream_key, axis), (), 0, length) for axis, length in enumerate(result.shape)]
    longest = result.shape.index(max(result.shape))
    next_to = spot[:longest] + [(spot[longest] + 1) % result.shape[longest]] + spot[longest + 1:]
    return result.at[tuple(spot)].set(least).at[tuple(next_to)].set(high)


def block_levels(rng, dims, split, low, largest):
    loudness, own = 1.0, jax.random.fold_in(rng, 6)
    for axis_at, parts in split:
        draws = jnp.exp(jax.random.uniform(jax.random.fold_in(own, axis_at), (parts,), jnp.float32, low / len(split), largest / len(split)))
        loudness = loudness * jnp.repeat(draws, dims[axis_at] // parts).reshape([-1 if axis == axis_at else 1 for axis in range(len(dims))])
    return loudness


def centred(key, extent, scale, most, shards=(), held_as=jnp.bfloat16):
    array = jax.random.normal(key, extent, jnp.float32) * scale
    if len(shards) > 0:
        array = block_levels(key, extent, shards, -0.22, 0.18) * array
    return jnp.clip(array, min=-most, max=most).astype(held_as)


def setup_inputs(seed: int = 0) -> dict:
    splits = jax.random.split(jax.random.key(seed), 6)
    return {
        "thermal_anomaly": centred(splits[0], (LAYER_TOTAL, PARALLEL_TOTAL, MERIDIAN_TOTAL), 1.0, 6.0, ((1, 4), (2, 8)), jnp.float32),
        "saltiness_anomaly": centred(splits[1], (LAYER_TOTAL, PARALLEL_TOTAL, MERIDIAN_TOTAL), 1.0, 6.0, ((1, 4), (2, 8)), jnp.float32),
        "zonal_velocity": centred(splits[2], (LAYER_TOTAL, PARALLEL_TOTAL, MERIDIAN_TOTAL), 0.5, 3.0, ((1, 4), (2, 8)), jnp.float32),
        "meridional_velocity": centred(splits[3], (LAYER_TOTAL, PARALLEL_TOTAL, MERIDIAN_TOTAL), 0.5, 3.0, ((1, 4), (2, 8)), jnp.float32),
        "sea_point_indicator": set_ends((jax.random.randint(splits[4], (LAYER_TOTAL, PARALLEL_TOTAL, MERIDIAN_TOTAL), 0, 4) < 3).astype(jnp.int32), jax.random.fold_in(splits[4], 1), 0, 1),
    }


time_step = 0.8
diffusivity = 0.15
pressure_gain = 0.12
layer_depth = 0.5


def hydrostatic_force(temp_field, salt_field):
    density = 0.8 * salt_field - 0.2 * temp_field
    return jnp.cumsum(density, axis=0) * layer_depth


def velocity(east_field, north_field, hydrostatic_load, sea_share_factor):
    grad_east = hydrostatic_load[:, 1:-1, 2:] - hydrostatic_load[:, 1:-1, :-2]
    grad_north = hydrostatic_load[:, 2:, 1:-1] - hydrostatic_load[:, :-2, 1:-1]
    zonal_velocity_next = (east_field - pressure_gain * grad_east) * sea_share_factor
    meridional_velocity_next = (north_field - pressure_gain * grad_north) * sea_share_factor
    return zonal_velocity_next, meridional_velocity_next


def advected_scalar(tracer_field, east_field, north_field, sea_share_factor):
    rows_q = tracer_field[:, 1:-1, :]
    rows_u = east_field[:, 1:-1, :]
    rows_m = sea_share_factor[:, 1:-1, :]
    flux_east = 0.25 * (rows_u[..., :-1] + rows_u[..., 1:]) * (rows_q[..., :-1] + rows_q[..., 1:])
    flux_east = (flux_east - diffusivity * (rows_q[..., 1:] - rows_q[..., :-1])) * rows_m[..., :-1] * rows_m[..., 1:]
    cols_q = tracer_field[:, :, 1:-1]
    cols_v = north_field[:, :, 1:-1]
    cols_m = sea_share_factor[:, :, 1:-1]
    flux_north = 0.25 * (cols_v[:, :-1] + cols_v[:, 1:]) * (cols_q[:, :-1] + cols_q[:, 1:])
    flux_north = (flux_north - diffusivity * (cols_q[:, 1:] - cols_q[:, :-1])) * cols_m[:, :-1] * cols_m[:, 1:]
    divergence = flux_east[..., 1:] - flux_east[..., :-1] + flux_north[:, 1:] - flux_north[:, :-1]
    return tracer_field[:, 1:-1, 1:-1] - time_step * sea_share_factor[:, 1:-1, 1:-1] * divergence


def enlarge_entire_domain(field, signs, margin):
    south = jnp.zeros((field.shape[0], margin, field.shape[2]), field.dtype)
    north = jnp.flip(field[:, field.shape[1] - margin:, :], axis=(1, 2)) * signs
    stacked = jnp.concatenate([south, field, north], axis=1)
    return jnp.concatenate([stacked[..., stacked.shape[2] - margin:], stacked, stacked[..., :margin]], axis=2)


def reference(thermal_anomaly, saltiness_anomaly, zonal_velocity, meridional_velocity, sea_point_indicator):
    sea_share_factor = enlarge_entire_domain(sea_point_indicator.astype(thermal_anomaly.dtype), 1.0, 2)
    inner_sea_indicator = sea_share_factor[:, 1:-1, 1:-1]
    for repeat in range(STEPS):
        thermal_enlarged = enlarge_entire_domain(thermal_anomaly, 1.0, 2)
        saline_extended = enlarge_entire_domain(saltiness_anomaly, 1.0, 2)
        east_ext = enlarge_entire_domain(zonal_velocity, -1.0, 2)
        north_ext = enlarge_entire_domain(meridional_velocity, -1.0, 2)
        hydrostatic_load = hydrostatic_force(thermal_enlarged, saline_extended)
        zonal_velocity_next, meridional_velocity_next = velocity(east_ext[:, 1:-1, 1:-1], north_ext[:, 1:-1, 1:-1], hydrostatic_load, inner_sea_indicator)
        thermal_anomaly = advected_scalar(thermal_enlarged[:, 1:-1, 1:-1], zonal_velocity_next, meridional_velocity_next, inner_sea_indicator)
        saltiness_anomaly = advected_scalar(saline_extended[:, 1:-1, 1:-1], zonal_velocity_next, meridional_velocity_next, inner_sea_indicator)
        zonal_velocity = zonal_velocity_next[:, 1:-1, 1:-1]
        meridional_velocity = meridional_velocity_next[:, 1:-1, 1:-1]
    return thermal_anomaly, saltiness_anomaly, zonal_velocity, meridional_velocity
```

```python
import functools

import jax
import jax.numpy as jnp
from jax import lax
from jax.experimental import pallas as pl
from jax.experimental.pallas import tpu as pltpu
from jax.sharding import PartitionSpec as P

STEPS = 2
TIME_STEP = 0.8
DIFFUSIVITY = 0.15
PRESSURE_GAIN = 0.12
LAYER_DEPTH = 0.5
HALO = 2 * STEPS
FIELDS = 5
MESH = pl.DeviceIdType.MESH


def lane_iota(shape):
    return lax.broadcasted_iota(jnp.int32, shape, len(shape) - 1)


def swap_lanes(x, bits):
    width = x.shape[-1]
    lane = lane_iota(x.shape)
    bit = 1
    while bit < width:
        if bits & bit:
            up = pltpu.roll(x, bit, x.ndim - 1)
            if 2 * bit == width:
                x = up
            else:
                x = jnp.where((lane & bit) != 0, up, pltpu.roll(x, width - bit, x.ndim - 1))
        bit *= 2
    return x


def blocks(first, count, size, body):
    number = (count + size - 1) // size

    def step(b, _):
        start = jnp.minimum(first + b * size, first + count - size)
        body(start)
        return 0

    lax.fori_loop(0, number, step, 0)


def pressure_pass(temp, salt, load, first, count, size):
    def body(start):
        rows = pl.ds(start, size)
        total = (0.8 * LAYER_DEPTH) * salt[rows] - (0.2 * LAYER_DEPTH) * temp[rows]
        level = lax.broadcasted_iota(jnp.int32, total.shape, 1)
        shift = 1
        while shift < total.shape[1]:
            total = total + jnp.where(level >= shift, pltpu.roll(total, shift, 1), 0.0)
            shift *= 2
        load[rows] = total

    blocks(first, count, size, body)


def velocity_pass(load, wet, east, north, east_to, north_to, first, count, size):
    def body(start):
        rows = pl.ds(start, size)
        here = load[rows]
        width = here.shape[2]
        sea = wet[rows]
        grad_east = pltpu.roll(here, width - 1, 2) - pltpu.roll(here, 1, 2)
        grad_north = load[pl.ds(start + 1, size)] - load[pl.ds(start - 1, size)]
        east_to[rows] = (east[rows] - PRESSURE_GAIN * grad_east) * sea
        north_to[rows] = (north[rows] - PRESSURE_GAIN * grad_north) * sea

    blocks(first, count, size, body)


def tracer_pass(tracers, wet, east, north, tracers_to, first, count, size):
    def body(start):
        rows = pl.ds(start, size)
        around = pl.ds(start - 1, size + 2)
        sea = wet[around]
        inner = sea[1:-1]
        width = sea.shape[2]
        flow = east[rows]
        both = inner * pltpu.roll(inner, width - 1, 2)
        mean = 0.25 * (flow + pltpu.roll(flow, width - 1, 2))
        east_here, east_next = (mean + DIFFUSIVITY) * both, (mean - DIFFUSIVITY) * both
        rise = north[around]
        both = sea[:-1] * sea[1:]
        mean = 0.25 * (rise[:-1] + rise[1:])
        north_here, north_next = (mean + DIFFUSIVITY) * both, (mean - DIFFUSIVITY) * both
        scale = TIME_STEP * inner
        for tracer, tracer_to in zip(tracers, tracers_to):
            q = tracer[around]
            mid = q[1:-1]
            flux_east = east_here * mid + east_next * pltpu.roll(mid, width - 1, 2)
            flux_north = north_here * q[:-1] + north_next * q[1:]
            spread = flux_east - pltpu.roll(flux_east, 1, 2) + (flux_north[1:] - flux_north[:-1])
            tracer_to[rows] = mid - scale * spread

    blocks(first, count, size, body)


def run_steps(ext, work, rows, size):
    every = rows + 2 * HALO
    load = work.at[0]
    wet = ext.at[4]
    held = [ext.at[f] for f in range(4)]
    for step in range(STEPS):
        to = [work.at[1 + 4 * step + f] for f in range(4)]
        edge = 2 * step
        pressure_pass(held[0], held[1], load, edge, every - 2 * edge, size)
        velocity_pass(load, wet, held[2], held[3], to[2], to[3], edge + 1, every - 2 * edge - 2, size)
        tracer_pass(held[:2], wet, to[2], to[3], to[:2], edge + 2, every - 2 * edge - 4, size)
        held = to


def kernel(
    rows,
    levels,
    temp_hbm,
    salt_hbm,
    east_hbm,
    north_hbm,
    wet_hbm,
    temp_out,
    salt_out,
    east_out,
    north_out,
    staged,
    staged_wet,
    ext,
    seam,
    main_work,
    seam_work,
    packed,
    from_left,
    from_right,
    merged,
    corner,
    load_sem,
    row_send,
    row_recv,
    col_send,
    col_recv,
    corner_send,
    corner_recv,
):
    lon, lat = lax.axis_index("lon"), lax.axis_index("lat")
    lon_total, lat_total = lax.axis_size("lon"), lax.axis_size("lat")
    at_top = lat == lat_total - 1
    has_south = lat > 0
    left, right = lax.rem(lon + lon_total - 1, lon_total), lax.rem(lon + 1, lon_total)
    top = (lat // (lat_total - 1)) if lat_total > 1 else 1
    north_lon = lon + top * (lon_total - 1 - 2 * lon)
    north_lat = lat + 1 - top
    north_id = {"lon": north_lon, "lat": north_lat}
    south_id = {"lon": lon, "lat": lat - 1}
    left_id, right_id = {"lon": left, "lat": lat}, {"lon": right, "lat": lat}

    inputs = (temp_hbm, salt_hbm, east_hbm, north_hbm)
    loads = [pltpu.make_async_copy(h, staged.at[f], load_sem.at[f]) for f, h in enumerate(inputs)]
    loads.append(pltpu.make_async_copy(wet_hbm, staged_wet, load_sem.at[4]))
    for copy in loads:
        copy.start()

    barrier = pltpu.get_barrier_semaphore()
    for other in (left_id, right_id, north_id):
        pl.semaphore_signal(barrier, inc=1, device_id=other, device_id_type=MESH)

    @pl.when(has_south)
    def _():
        pl.semaphore_signal(barrier, inc=1, device_id=south_id, device_id_type=MESH)

    for f in range(FIELDS):
        loads[f].wait()
        for r in range(rows):
            if f < 4:
                value = staged[f, pl.ds(r, levels, stride=rows), :]
            else:
                value = staged_wet[pl.ds(r, levels, stride=rows), :].astype(jnp.float32)
            ext[f, HALO + r] = value

    pl.semaphore_wait(barrier, 3 + jnp.minimum(lat, 1))

    north_base = HALO + rows
    row_north = pltpu.make_async_remote_copy(
        src_ref=ext.at[:, pl.ds(rows, HALO)],
        dst_ref=ext.at[:, pl.ds(top * north_base, HALO)],
        send_sem=row_send.at[0],
        recv_sem=row_recv.at[top],
        device_id=north_id,
        device_id_type=MESH,
    )
    row_south = pltpu.make_async_remote_copy(
        src_ref=ext.at[:, pl.ds(HALO, HALO)],
        dst_ref=ext.at[:, pl.ds(north_base, HALO)],
        send_sem=row_send.at[1],
        recv_sem=row_recv.at[1],
        device_id=south_id,
        device_id_type=MESH,
    )
    row_north.start()

    @pl.when(has_south)
    def _():
        row_south.start()

    width = ext.shape[-1]
    slot_lanes = 2 * HALO
    groups = rows // HALO
    gathered = jnp.zeros((groups, levels, width), jnp.float32)
    slot_of = lane_iota(gathered.shape) // slot_lanes
    for f in range(4):
        block = ext[f, HALO : HALO + rows].reshape(groups, HALO, levels, width)
        for i in range(HALO):
            slot = HALO * f + i
            turned = pltpu.roll(block[:, i], (HALO + slot_lanes * slot) % width, 2)
            gathered = jnp.where(slot_of == slot, turned, gathered)
    packed[1 : 1 + groups] = gathered
    slots = width // slot_lanes
    halves = jnp.zeros((2, levels, width), jnp.float32)
    slot_of = lane_iota(halves.shape) // slot_lanes
    block = ext[4, HALO : HALO + rows].reshape(2, slots, levels, width)
    for slot in range(slots):
        turned = pltpu.roll(block[:, slot], (HALO + slot_lanes * slot) % width, 2)
        halves = jnp.where(slot_of == slot, turned, halves)
    packed[0] = halves[0]
    packed[1 + groups] = halves[1]

    to_left = pltpu.make_async_remote_copy(
        src_ref=packed,
        dst_ref=from_right,
        send_sem=col_send.at[0],
        recv_sem=col_recv.at[1],
        device_id=left_id,
        device_id_type=MESH,
    )
    to_right = pltpu.make_async_remote_copy(
        src_ref=packed,
        dst_ref=from_left,
        send_sem=col_send.at[1],
        recv_sem=col_recv.at[0],
        device_id=right_id,
        device_id_type=MESH,
    )
    to_left.start()
    to_right.start()

    @pl.when(lat == 0)
    def _():
        ext[:, 0:HALO] = jnp.zeros((FIELDS, HALO, levels, width), jnp.float32)
        corner[0] = jnp.zeros((2, levels, width), jnp.float32)

    to_left.wait_recv()
    to_right.wait_recv()
    before, after = from_left[...], from_right[...]
    lane = lane_iota(before.shape)
    merged[...] = jnp.where(
        (lane & HALO) != 0, pltpu.roll(before, HALO, 2), pltpu.roll(after, width - HALO, 2)
    )

    corner_north = pltpu.make_async_remote_copy(
        src_ref=merged.at[pl.ds(groups, 2)],
        dst_ref=corner.at[top],
        send_sem=corner_send.at[0],
        recv_sem=corner_recv.at[top],
        device_id=north_id,
        device_id_type=MESH,
    )
    corner_south = pltpu.make_async_remote_copy(
        src_ref=merged.at[pl.ds(0, 2)],
        dst_ref=corner.at[1],
        send_sem=corner_send.at[1],
        recv_sem=corner_recv.at[1],
        device_id=south_id,
        device_id_type=MESH,
    )
    corner_north.start()

    @pl.when(has_south)
    def _():
        corner_south.start()

    row_south.wait_recv()

    @pl.when(has_south)
    def _():
        pltpu.make_async_remote_copy(
            src_ref=ext.at[:, pl.ds(rows, HALO)],
            dst_ref=ext.at[:, pl.ds(0, HALO)],
            send_sem=row_send.at[0],
            recv_sem=row_recv.at[0],
            device_id=north_id,
            device_id_type=MESH,
        ).wait_recv()

    @pl.when(at_top)
    def _():
        for f in range(FIELDS):
            turned = swap_lanes(ext[f, north_base : north_base + HALO], width - 1)
            if f in (2, 3):
                turned = -turned
            for i in range(HALO):
                ext[f, north_base + i] = turned[HALO - 1 - i]

    run_steps(ext, main_work, rows, 4)

    def stitch(own, piece, slot):
        spot = lane_iota(own.shape)
        edges = pltpu.roll(piece, (width - slot_lanes * (slot + 1)) % width, own.ndim - 1)
        value = jnp.where(spot < width // 2, own, pltpu.roll(own, width - slot_lanes, own.ndim - 1))
        return jnp.where(spot >= width - slot_lanes, edges, value)

    center = merged[1 : 1 + groups]
    for f in range(4):
        block = ext[f, HALO : HALO + rows].reshape(groups, HALO, levels, width)
        for i in range(HALO):
            value = stitch(block[:, i], center, HALO * f + i)
            for g in range(groups):
                seam[f, HALO + HALO * g + i] = value[g]
    for half in range(2):
        piece = merged[half * (1 + groups)]
        for slot in range(slots):
            r = HALO + slots * half + slot
            seam[4, r] = stitch(ext[4, r], piece, slot)

    corner_south.wait_recv()

    @pl.when(has_south)
    def _():
        pltpu.make_async_remote_copy(
            src_ref=merged.at[pl.ds(groups, 2)],
            dst_ref=corner.at[0],
            send_sem=corner_send.at[0],
            recv_sem=corner_recv.at[0],
            device_id=north_id,
            device_id_type=MESH,
        ).wait_recv()

    @pl.when(at_top)
    def _():
        fields = swap_lanes(corner[1, 0], slot_lanes * HALO - 1)
        fields = jnp.where(lane_iota(fields.shape) >= width // 2, -fields, fields)
        sea = swap_lanes(corner[1, 1], width - 1)
        corner[1, 0] = sea
        corner[1, 1] = fields

    for side in range(2):
        fields, sea = corner[side, side], corner[side, 1 - side]
        base = side * north_base
        for i in range(HALO):
            for f in range(4):
                seam[f, base + i] = stitch(ext[f, base + i], fields, HALO * f + i)
            slot = i if side else slots - HALO + i
            seam[4, base + i] = stitch(ext[4, base + i], sea, slot)

    run_steps(seam, seam_work, rows, 4)

    for f, out in enumerate((temp_out, salt_out, east_out, north_out)):
        for r in range(rows):
            edge = seam_work[5 + f, HALO + r]
            spot = lane_iota(edge.shape)
            value = main_work[5 + f, HALO + r]
            value = jnp.where(spot < HALO, edge, value)
            value = jnp.where(spot >= width - HALO, pltpu.roll(edge, slot_lanes, 1), value)
            out[pl.ds(r, levels, stride=rows), :] = value

    row_north.wait_send()
    to_left.wait_send()
    to_right.wait_send()
    corner_north.wait_send()

    @pl.when(has_south)
    def _():
        row_south.wait_send()
        corner_south.wait_send()


def shards(temp, salt, east, north, wet):
    levels, rows, columns = temp.shape
    flat = [x.reshape(levels * rows, columns) for x in (temp, salt, east, north, wet)]
    every = rows + 2 * HALO
    pieces = rows // HALO + 2
    plane = (levels, columns)
    vmem = lambda *lead: pltpu.VMEM(lead + plane, jnp.float32)
    outs = pl.pallas_call(
        functools.partial(kernel, rows, levels),
        out_shape=[jax.ShapeDtypeStruct((levels * rows, columns), jnp.float32)] * 4,
        in_specs=[pl.BlockSpec(memory_space=pl.ANY)] * 5,
        out_specs=[pl.BlockSpec(memory_space=pltpu.VMEM)] * 4,
        scratch_shapes=[
            pltpu.VMEM((4, levels * rows, columns), jnp.float32),
            pltpu.VMEM((levels * rows, columns), jnp.int32),
            vmem(FIELDS, every),
            vmem(FIELDS, every),
            vmem(9, every),
            vmem(9, every),
            vmem(pieces),
            vmem(pieces),
            vmem(pieces),
            vmem(pieces),
            vmem(2, 2),
            pltpu.SemaphoreType.DMA((FIELDS,)),
            pltpu.SemaphoreType.DMA((2,)),
            pltpu.SemaphoreType.DMA((2,)),
            pltpu.SemaphoreType.DMA((2,)),
            pltpu.SemaphoreType.DMA((2,)),
            pltpu.SemaphoreType.DMA((2,)),
            pltpu.SemaphoreType.DMA((2,)),
        ],
        compiler_params=pltpu.CompilerParams(
            collective_id=0, has_side_effects=True, vmem_limit_bytes=60 * 1024 * 1024
        ),
    )(*flat)
    return tuple(x.reshape(levels, rows, columns) for x in outs)


def solution(mesh):
    spec = P(None, "lat", "lon")
    return jax.shard_map(
        shards, mesh=mesh, in_specs=(spec,) * 5, out_specs=(spec,) * 4, check_vma=False
    )
```

```python
import functools

import jax
import jax.numpy as jnp
from jax import lax
from jax.experimental import pallas as pl
from jax.experimental.pallas import tpu as pltpu
from jax.sharding import PartitionSpec as P

STEPS = 2
TIME_STEP = 0.8
DIFFUSIVITY = 0.15
PRESSURE_GAIN = 0.12
LAYER_DEPTH = 0.5
HALO = 2 * STEPS
FIELDS = 5
MESH = pl.DeviceIdType.MESH


def lane_iota(shape):
    return lax.broadcasted_iota(jnp.int32, shape, len(shape) - 1)


def swap_lanes(x, bits):
    width = x.shape[-1]
    lane = lane_iota(x.shape)
    bit = 1
    while bit < width:
        if bits & bit:
            up = pltpu.roll(x, bit, x.ndim - 1)
            if 2 * bit == width:
                x = up
            else:
                x = jnp.where((lane & bit) != 0, up, pltpu.roll(x, width - bit, x.ndim - 1))
        bit *= 2
    return x


def blocks(first, count, size, body):
    number = (count + size - 1) // size

    for b in range(number):
        body(min(first + b * size, first + count - size))


def pressure_pass(temp, salt, load, first, count, size):
    def body(start):
        rows = pl.ds(start, size)
        total = (0.8 * LAYER_DEPTH) * salt[rows] - (0.2 * LAYER_DEPTH) * temp[rows]
        level = lax.broadcasted_iota(jnp.int32, total.shape, 1)
        shift = 1
        while shift < total.shape[1]:
            total = total + jnp.where(level >= shift, pltpu.roll(total, shift, 1), 0.0)
            shift *= 2
        load[rows] = total

    blocks(first, count, size, body)


def velocity_pass(load, wet, east, north, east_to, north_to, first, count, size):
    def body(start):
        rows = pl.ds(start, size)
        here = load[rows]
        width = here.shape[2]
        sea = wet[rows]
        grad_east = pltpu.roll(here, width - 1, 2) - pltpu.roll(here, 1, 2)
        grad_north = load[pl.ds(start + 1, size)] - load[pl.ds(start - 1, size)]
        east_to[rows] = (east[rows] - PRESSURE_GAIN * grad_east) * sea
        north_to[rows] = (north[rows] - PRESSURE_GAIN * grad_north) * sea

    blocks(first, count, size, body)


def tracer_pass(tracers, wet, east, north, tracers_to, first, count, size):
    def body(start):
        rows = pl.ds(start, size)
        around = pl.ds(start - 1, size + 2)
        sea = wet[around]
        inner = sea[1:-1]
        width = sea.shape[2]
        flow = east[rows]
        both = inner * pltpu.roll(inner, width - 1, 2)
        mean = 0.25 * (flow + pltpu.roll(flow, width - 1, 2))
        east_here, east_next = (mean + DIFFUSIVITY) * both, (mean - DIFFUSIVITY) * both
        rise = north[around]
        both = sea[:-1] * sea[1:]
        mean = 0.25 * (rise[:-1] + rise[1:])
        north_here, north_next = (mean + DIFFUSIVITY) * both, (mean - DIFFUSIVITY) * both
        scale = TIME_STEP * inner
        for tracer, tracer_to in zip(tracers, tracers_to):
            q = tracer[around]
            mid = q[1:-1]
            flux_east = east_here * mid + east_next * pltpu.roll(mid, width - 1, 2)
            flux_north = north_here * q[:-1] + north_next * q[1:]
            spread = flux_east - pltpu.roll(flux_east, 1, 2) + (flux_north[1:] - flux_north[:-1])
            tracer_to[rows] = mid - scale * spread

    blocks(first, count, size, body)


def run_steps(ext, work, rows, size):
    every = rows + 2 * HALO
    load = work.at[0]
    wet = ext.at[4]
    held = [ext.at[f] for f in range(4)]
    for step in range(STEPS):
        to = [work.at[1 + 4 * step + f] for f in range(4)]
        edge = 2 * step
        pressure_pass(held[0], held[1], load, edge, every - 2 * edge, size)
        velocity_pass(load, wet, held[2], held[3], to[2], to[3], edge + 1, every - 2 * edge - 2, size)
        tracer_pass(held[:2], wet, to[2], to[3], to[:2], edge + 2, every - 2 * edge - 4, size)
        held = to


def kernel(
    rows,
    levels,
    temp_hbm,
    salt_hbm,
    east_hbm,
    north_hbm,
    wet_hbm,
    temp_out,
    salt_out,
    east_out,
    north_out,
    staged,
    staged_wet,
    ext,
    seam,
    main_work,
    seam_work,
    packed,
    from_left,
    from_right,
    merged,
    corner,
    load_sem,
    row_send,
    row_recv,
    col_send,
    col_recv,
    corner_send,
    corner_recv,
):
    lon, lat = lax.axis_index("lon"), lax.axis_index("lat")
    lon_total, lat_total = lax.axis_size("lon"), lax.axis_size("lat")
    at_top = lat == lat_total - 1
    has_south = lat > 0
    left, right = lax.rem(lon + lon_total - 1, lon_total), lax.rem(lon + 1, lon_total)
    top = (lat // (lat_total - 1)) if lat_total > 1 else 1
    north_lon = lon + top * (lon_total - 1 - 2 * lon)
    north_lat = lat + 1 - top
    north_id = {"lon": north_lon, "lat": north_lat}
    south_id = {"lon": lon, "lat": lat - 1}
    left_id, right_id = {"lon": left, "lat": lat}, {"lon": right, "lat": lat}

    inputs = (temp_hbm, salt_hbm, east_hbm, north_hbm)
    loads = [pltpu.make_async_copy(h, staged.at[f], load_sem.at[f]) for f, h in enumerate(inputs)]
    loads.append(pltpu.make_async_copy(wet_hbm, staged_wet, load_sem.at[4]))
    for copy in loads:
        copy.start()

    barrier = pltpu.get_barrier_semaphore()
    for other in (left_id, right_id, north_id):
        pl.semaphore_signal(barrier, inc=1, device_id=other, device_id_type=MESH)

    @pl.when(has_south)
    def _():
        pl.semaphore_signal(barrier, inc=1, device_id=south_id, device_id_type=MESH)

    for f in range(FIELDS):
        loads[f].wait()
        for r in range(rows):
            if f < 4:
                value = staged[f, pl.ds(r, levels, stride=rows), :]
            else:
                value = staged_wet[pl.ds(r, levels, stride=rows), :].astype(jnp.float32)
            ext[f, HALO + r] = value

    pl.semaphore_wait(barrier, 3 + jnp.minimum(lat, 1))

    north_base = HALO + rows
    row_north = pltpu.make_async_remote_copy(
        src_ref=ext.at[:, pl.ds(rows, HALO)],
        dst_ref=ext.at[:, pl.ds(top * north_base, HALO)],
        send_sem=row_send.at[0],
        recv_sem=row_recv.at[top],
        device_id=north_id,
        device_id_type=MESH,
    )
    row_south = pltpu.make_async_remote_copy(
        src_ref=ext.at[:, pl.ds(HALO, HALO)],
        dst_ref=ext.at[:, pl.ds(north_base, HALO)],
        send_sem=row_send.at[1],
        recv_sem=row_recv.at[1],
        device_id=south_id,
        device_id_type=MESH,
    )
    row_north.start()

    @pl.when(has_south)
    def _():
        row_south.start()

    width = ext.shape[-1]
    slot_lanes = 2 * HALO
    groups = rows // HALO
    gathered = jnp.zeros((groups, levels, width), jnp.float32)
    slot_of = lane_iota(gathered.shape) // slot_lanes
    for f in range(4):
        block = ext[f, HALO : HALO + rows].reshape(groups, HALO, levels, width)
        for i in range(HALO):
            slot = HALO * f + i
            turned = pltpu.roll(block[:, i], (HALO + slot_lanes * slot) % width, 2)
            gathered = jnp.where(slot_of == slot, turned, gathered)
    packed[1 : 1 + groups] = gathered
    slots = width // slot_lanes
    halves = jnp.zeros((2, levels, width), jnp.float32)
    slot_of = lane_iota(halves.shape) // slot_lanes
    block = ext[4, HALO : HALO + rows].reshape(2, slots, levels, width)
    for slot in range(slots):
        turned = pltpu.roll(block[:, slot], (HALO + slot_lanes * slot) % width, 2)
        halves = jnp.where(slot_of == slot, turned, halves)
    packed[0] = halves[0]
    packed[1 + groups] = halves[1]

    to_left = pltpu.make_async_remote_copy(
        src_ref=packed,
        dst_ref=from_right,
        send_sem=col_send.at[0],
        recv_sem=col_recv.at[1],
        device_id=left_id,
        device_id_type=MESH,
    )
    to_right = pltpu.make_async_remote_copy(
        src_ref=packed,
        dst_ref=from_left,
        send_sem=col_send.at[1],
        recv_sem=col_recv.at[0],
        device_id=right_id,
        device_id_type=MESH,
    )
    to_left.start()
    to_right.start()

    @pl.when(lat == 0)
    def _():
        ext[:, 0:HALO] = jnp.zeros((FIELDS, HALO, levels, width), jnp.float32)
        corner[0] = jnp.zeros((2, levels, width), jnp.float32)

    to_left.wait_recv()
    to_right.wait_recv()
    before, after = from_left[...], from_right[...]
    lane = lane_iota(before.shape)
    merged[...] = jnp.where(
        (lane & HALO) != 0, pltpu.roll(before, HALO, 2), pltpu.roll(after, width - HALO, 2)
    )

    corner_north = pltpu.make_async_remote_copy(
        src_ref=merged.at[pl.ds(groups, 2)],
        dst_ref=corner.at[top],
        send_sem=corner_send.at[0],
        recv_sem=corner_recv.at[top],
        device_id=north_id,
        device_id_type=MESH,
    )
    corner_south = pltpu.make_async_remote_copy(
        src_ref=merged.at[pl.ds(0, 2)],
        dst_ref=corner.at[1],
        send_sem=corner_send.at[1],
        recv_sem=corner_recv.at[1],
        device_id=south_id,
        device_id_type=MESH,
    )
    corner_north.start()

    @pl.when(has_south)
    def _():
        corner_south.start()

    row_south.wait_recv()

    @pl.when(has_south)
    def _():
        pltpu.make_async_remote_copy(
            src_ref=ext.at[:, pl.ds(rows, HALO)],
            dst_ref=ext.at[:, pl.ds(0, HALO)],
            send_sem=row_send.at[0],
            recv_sem=row_recv.at[0],
            device_id=north_id,
            device_id_type=MESH,
        ).wait_recv()

    @pl.when(at_top)
    def _():
        for f in range(FIELDS):
            turned = swap_lanes(ext[f, north_base : north_base + HALO], width - 1)
            if f in (2, 3):
                turned = -turned
            for i in range(HALO):
                ext[f, north_base + i] = turned[HALO - 1 - i]

    run_steps(ext, main_work, rows, 8)

    def stitch(own, piece, slot):
        spot = lane_iota(own.shape)
        edges = pltpu.roll(piece, (width - slot_lanes * (slot + 1)) % width, own.ndim - 1)
        value = jnp.where(spot < width // 2, own, pltpu.roll(own, width - slot_lanes, own.ndim - 1))
        return jnp.where(spot >= width - slot_lanes, edges, value)

    center = merged[1 : 1 + groups]
    for f in range(4):
        block = ext[f, HALO : HALO + rows].reshape(groups, HALO, levels, width)
        for i in range(HALO):
            value = stitch(block[:, i], center, HALO * f + i)
            for g in range(groups):
                seam[f, HALO + HALO * g + i] = value[g]
    for half in range(2):
        piece = merged[half * (1 + groups)]
        for slot in range(slots):
            r = HALO + slots * half + slot
            seam[4, r] = stitch(ext[4, r], piece, slot)

    corner_south.wait_recv()

    @pl.when(has_south)
    def _():
        pltpu.make_async_remote_copy(
            src_ref=merged.at[pl.ds(groups, 2)],
            dst_ref=corner.at[0],
            send_sem=corner_send.at[0],
            recv_sem=corner_recv.at[0],
            device_id=north_id,
            device_id_type=MESH,
        ).wait_recv()

    @pl.when(at_top)
    def _():
        fields = swap_lanes(corner[1, 0], slot_lanes * HALO - 1)
        fields = jnp.where(lane_iota(fields.shape) >= width // 2, -fields, fields)
        sea = swap_lanes(corner[1, 1], width - 1)
        corner[1, 0] = sea
        corner[1, 1] = fields

    for side in range(2):
        fields, sea = corner[side, side], corner[side, 1 - side]
        base = side * north_base
        for i in range(HALO):
            for f in range(4):
                seam[f, base + i] = stitch(ext[f, base + i], fields, HALO * f + i)
            slot = i if side else slots - HALO + i
            seam[4, base + i] = stitch(ext[4, base + i], sea, slot)

    run_steps(seam, seam_work, rows, 8)

    for f, out in enumerate((temp_out, salt_out, east_out, north_out)):
        for r in range(rows):
            edge = seam_work[5 + f, HALO + r]
            spot = lane_iota(edge.shape)
            value = main_work[5 + f, HALO + r]
            value = jnp.where(spot < HALO, edge, value)
            value = jnp.where(spot >= width - HALO, pltpu.roll(edge, slot_lanes, 1), value)
            out[pl.ds(r, levels, stride=rows), :] = value

    row_north.wait_send()
    to_left.wait_send()
    to_right.wait_send()
    corner_north.wait_send()

    @pl.when(has_south)
    def _():
        row_south.wait_send()
        corner_south.wait_send()


def write_out(*refs):
    count = (len(refs) - 1) // 2
    sems = refs[-1]
    copies = [
        pltpu.make_async_copy(refs[f], refs[count + f], sems.at[f]) for f in range(count)
    ]
    for copy in copies:
        copy.start()
    for copy in copies:
        copy.wait()


def shards(temp, salt, east, north, wet):
    levels, rows, columns = temp.shape
    flat = [x.reshape(levels * rows, columns) for x in (temp, salt, east, north, wet)]
    every = rows + 2 * HALO
    pieces = rows // HALO + 2
    plane = (levels, columns)
    vmem = lambda *lead: pltpu.VMEM(lead + plane, jnp.float32)
    flat = [pltpu.with_memory_space_constraint(x, pltpu.HBM) for x in flat]
    outs = pl.pallas_call(
        functools.partial(kernel, rows, levels),
        out_shape=[pltpu.VMEM((levels * rows, columns), jnp.float32)] * 4,
        in_specs=[pl.BlockSpec(memory_space=pltpu.HBM)] * 5,
        out_specs=[pl.BlockSpec(memory_space=pltpu.VMEM)] * 4,
        scratch_shapes=[
            pltpu.VMEM((4, levels * rows, columns), jnp.float32),
            pltpu.VMEM((levels * rows, columns), jnp.int32),
            vmem(FIELDS, every),
            vmem(FIELDS, every),
            vmem(9, every),
            vmem(9, every),
            vmem(pieces),
            vmem(pieces),
            vmem(pieces),
            vmem(pieces),
            vmem(2, 2),
            pltpu.SemaphoreType.DMA((FIELDS,)),
            pltpu.SemaphoreType.DMA((2,)),
            pltpu.SemaphoreType.DMA((2,)),
            pltpu.SemaphoreType.DMA((2,)),
            pltpu.SemaphoreType.DMA((2,)),
            pltpu.SemaphoreType.DMA((2,)),
            pltpu.SemaphoreType.DMA((2,)),
        ],
        compiler_params=pltpu.CompilerParams(
            collective_id=0, has_side_effects=True, vmem_limit_bytes=16 * 1024 * 1024
        ),
    )(*flat)
    outs = pl.pallas_call(
        write_out,
        out_shape=[jax.ShapeDtypeStruct((levels * rows, columns), jnp.float32)] * 4,
        in_specs=[pl.BlockSpec(memory_space=pltpu.VMEM)] * 4,
        out_specs=[pl.BlockSpec(memory_space=pltpu.HBM)] * 4,
        scratch_shapes=[pltpu.SemaphoreType.DMA((4,))],
        compiler_params=pltpu.CompilerParams(vmem_limit_bytes=2 * 1024 * 1024),
    )(*outs)
    return tuple(x.reshape(levels, rows, columns) for x in outs)


def solution(mesh):
    spec = P(None, "lat", "lon")
    return jax.shard_map(
        shards, mesh=mesh, in_specs=(spec,) * 5, out_specs=(spec,) * 4, check_vma=False
    )
```

```python
import functools

import jax
import jax.numpy as jnp
from jax import lax
from jax.experimental import pallas as pl
from jax.experimental.pallas import tpu as pltpu
from jax.sharding import PartitionSpec as P

STEPS = 2
TIME_STEP = 0.8
DIFFUSIVITY = 0.15
PRESSURE_GAIN = 0.12
LAYER_DEPTH = 0.5
HALO = 2 * STEPS
FIELDS = 5
MESH = pl.DeviceIdType.MESH


def lane_iota(shape):
    return lax.broadcasted_iota(jnp.int32, shape, len(shape) - 1)


def swap_lanes(x, bits):
    width = x.shape[-1]
    lane = lane_iota(x.shape)
    bit = 1
    while bit < width:
        if bits & bit:
            up = pltpu.roll(x, bit, x.ndim - 1)
            if 2 * bit == width:
                x = up
            else:
                x = jnp.where((lane & bit) != 0, up, pltpu.roll(x, width - bit, x.ndim - 1))
        bit *= 2
    return x


def blocks(first, count, size, body):
    start = first
    while start < first + count:
        body(start, min(size, first + count - start))
        start += size


def pressure_pass(temp, salt, load, first, count, size):
    def body(start, size):
        rows = pl.ds(start, size)
        total = (0.8 * LAYER_DEPTH) * salt[rows] - (0.2 * LAYER_DEPTH) * temp[rows]
        level = lax.broadcasted_iota(jnp.int32, total.shape, 1)
        shift = 1
        while shift < total.shape[1]:
            total = total + jnp.where(level >= shift, pltpu.roll(total, shift, 1), 0.0)
            shift *= 2
        load[rows] = total

    blocks(first, count, size, body)


def velocity_pass(load, wet, east, north, east_to, north_to, first, count, size):
    def body(start, size):
        rows = pl.ds(start, size)
        here = load[rows]
        width = here.shape[2]
        sea = wet[rows]
        grad_east = pltpu.roll(here, width - 1, 2) - pltpu.roll(here, 1, 2)
        grad_north = load[pl.ds(start + 1, size)] - load[pl.ds(start - 1, size)]
        east_to[rows] = (east[rows] - PRESSURE_GAIN * grad_east) * sea
        north_to[rows] = (north[rows] - PRESSURE_GAIN * grad_north) * sea

    blocks(first, count, size, body)


def tracer_pass(tracers, wet, east, north, tracers_to, first, count, size):
    def body(start, size):
        rows = pl.ds(start, size)
        around = pl.ds(start - 1, size + 2)
        sea = wet[around]
        inner = sea[1:-1]
        width = sea.shape[2]
        flow = east[rows]
        both = inner * pltpu.roll(inner, width - 1, 2)
        mean = 0.25 * (flow + pltpu.roll(flow, width - 1, 2))
        east_here, east_next = (mean + DIFFUSIVITY) * both, (mean - DIFFUSIVITY) * both
        rise = north[around]
        both = sea[:-1] * sea[1:]
        mean = 0.25 * (rise[:-1] + rise[1:])
        north_here, north_next = (mean + DIFFUSIVITY) * both, (mean - DIFFUSIVITY) * both
        scale = TIME_STEP * inner
        for tracer, tracer_to in zip(tracers, tracers_to):
            q = tracer[around]
            mid = q[1:-1]
            flux_east = east_here * mid + east_next * pltpu.roll(mid, width - 1, 2)
            flux_north = north_here * q[:-1] + north_next * q[1:]
            spread = flux_east - pltpu.roll(flux_east, 1, 2) + (flux_north[1:] - flux_north[:-1])
            tracer_to[rows] = mid - scale * spread

    blocks(first, count, size, body)


def run_steps(ext, work, rows, size, parts):
    every = rows + 2 * HALO
    wet = ext.at[4]
    held = [ext.at[f] for f in range(4)]
    for step in range(STEPS):
        load = work.at[9 * step]
        to = [work.at[1 + 4 * step + f] for f in range(4)]
        for reach in range(3):
            edge = 2 * step + reach
            whole = (edge, every - 2 * edge)
            inner = (edge + HALO, every - 2 * edge - 2 * HALO)
            outer = [(edge, HALO), (every - edge - HALO, HALO)]
            todo = {"inner": [inner], "outer": outer, "whole": [whole]}[parts]
            for first, count in todo:
                if reach == 0:
                    pressure_pass(held[0], held[1], load, first, count, size)
                elif reach == 1:
                    velocity_pass(load, wet, held[2], held[3], to[2], to[3], first, count, size)
                else:
                    tracer_pass(held[:2], wet, to[2], to[3], to[:2], first, count, size)
        held = to


def kernel(
    rows,
    levels,
    temp_hbm,
    salt_hbm,
    east_hbm,
    north_hbm,
    wet_hbm,
    temp_out,
    salt_out,
    east_out,
    north_out,
    staged,
    staged_wet,
    ext,
    seam,
    main_work,
    seam_work,
    packed,
    from_left,
    from_right,
    merged,
    corner,
    load_sem,
    row_send,
    row_recv,
    col_send,
    col_recv,
    corner_send,
    corner_recv,
):
    lon, lat = lax.axis_index("lon"), lax.axis_index("lat")
    lon_total, lat_total = lax.axis_size("lon"), lax.axis_size("lat")
    at_top = lat == lat_total - 1
    has_south = lat > 0
    left, right = lax.rem(lon + lon_total - 1, lon_total), lax.rem(lon + 1, lon_total)
    top = (lat // (lat_total - 1)) if lat_total > 1 else 1
    north_lon = lon + top * (lon_total - 1 - 2 * lon)
    north_lat = lat + 1 - top
    north_id = {"lon": north_lon, "lat": north_lat}
    south_id = {"lon": lon, "lat": lat - 1}
    left_id, right_id = {"lon": left, "lat": lat}, {"lon": right, "lat": lat}

    inputs = (temp_hbm, salt_hbm, east_hbm, north_hbm)
    loads = [pltpu.make_async_copy(h, staged.at[f], load_sem.at[f]) for f, h in enumerate(inputs)]
    loads.append(pltpu.make_async_copy(wet_hbm, staged_wet, load_sem.at[4]))
    for copy in loads:
        copy.start()

    barrier = pltpu.get_barrier_semaphore()
    for other in (left_id, right_id, north_id):
        pl.semaphore_signal(barrier, inc=1, device_id=other, device_id_type=MESH)

    @pl.when(has_south)
    def _():
        pl.semaphore_signal(barrier, inc=1, device_id=south_id, device_id_type=MESH)

    for f in range(FIELDS):
        loads[f].wait()
        for r in range(rows):
            if f < 4:
                value = staged[f, pl.ds(r, levels, stride=rows), :]
            else:
                value = staged_wet[pl.ds(r, levels, stride=rows), :].astype(jnp.float32)
            ext[f, HALO + r] = value

    width = ext.shape[-1]
    slot_lanes = 2 * HALO
    groups = rows // HALO
    gathered = jnp.zeros((groups, levels, width), jnp.float32)
    slot_of = lane_iota(gathered.shape) // slot_lanes
    for f in range(4):
        block = ext[f, HALO : HALO + rows].reshape(groups, HALO, levels, width)
        for i in range(HALO):
            slot = HALO * f + i
            turned = pltpu.roll(block[:, i], (HALO + slot_lanes * slot) % width, 2)
            gathered = jnp.where(slot_of == slot, turned, gathered)
    packed[1 : 1 + groups] = gathered
    slots = width // slot_lanes
    halves = jnp.zeros((2, levels, width), jnp.float32)
    slot_of = lane_iota(halves.shape) // slot_lanes
    block = ext[4, HALO : HALO + rows].reshape(2, slots, levels, width)
    for slot in range(slots):
        turned = pltpu.roll(block[:, slot], (HALO + slot_lanes * slot) % width, 2)
        halves = jnp.where(slot_of == slot, turned, halves)
    packed[0] = halves[0]
    packed[1 + groups] = halves[1]

    pl.semaphore_wait(barrier, 3 + jnp.minimum(lat, 1))

    north_base = HALO + rows
    row_north = pltpu.make_async_remote_copy(
        src_ref=ext.at[:, pl.ds(rows, HALO)],
        dst_ref=ext.at[:, pl.ds(top * north_base, HALO)],
        send_sem=row_send.at[0],
        recv_sem=row_recv.at[top],
        device_id=north_id,
        device_id_type=MESH,
    )
    row_south = pltpu.make_async_remote_copy(
        src_ref=ext.at[:, pl.ds(HALO, HALO)],
        dst_ref=ext.at[:, pl.ds(north_base, HALO)],
        send_sem=row_send.at[1],
        recv_sem=row_recv.at[1],
        device_id=south_id,
        device_id_type=MESH,
    )
    to_left = pltpu.make_async_remote_copy(
        src_ref=packed,
        dst_ref=from_right,
        send_sem=col_send.at[0],
        recv_sem=col_recv.at[1],
        device_id=left_id,
        device_id_type=MESH,
    )
    to_right = pltpu.make_async_remote_copy(
        src_ref=packed,
        dst_ref=from_left,
        send_sem=col_send.at[1],
        recv_sem=col_recv.at[0],
        device_id=right_id,
        device_id_type=MESH,
    )

    to_left.start()
    to_right.start()
    row_north.start()

    @pl.when(has_south)
    def _():
        row_south.start()

    @pl.when(lat == 0)
    def _():
        ext[:, 0:HALO] = jnp.zeros((FIELDS, HALO, levels, width), jnp.float32)
        corner[0] = jnp.zeros((2, levels, width), jnp.float32)

    run_steps(ext, main_work, rows, 8, "inner")

    to_left.wait_recv()
    to_right.wait_recv()
    before, after = from_left[...], from_right[...]
    lane = lane_iota(before.shape)
    merged[...] = jnp.where(
        (lane & HALO) != 0, pltpu.roll(before, HALO, 2), pltpu.roll(after, width - HALO, 2)
    )

    corner_north = pltpu.make_async_remote_copy(
        src_ref=merged.at[pl.ds(groups, 2)],
        dst_ref=corner.at[top],
        send_sem=corner_send.at[0],
        recv_sem=corner_recv.at[top],
        device_id=north_id,
        device_id_type=MESH,
    )
    corner_south = pltpu.make_async_remote_copy(
        src_ref=merged.at[pl.ds(0, 2)],
        dst_ref=corner.at[1],
        send_sem=corner_send.at[1],
        recv_sem=corner_recv.at[1],
        device_id=south_id,
        device_id_type=MESH,
    )
    corner_north.start()

    @pl.when(has_south)
    def _():
        corner_south.start()

    def stitch(own, piece, slot):
        spot = lane_iota(own.shape)
        edges = pltpu.roll(piece, (width - slot_lanes * (slot + 1)) % width, own.ndim - 1)
        value = jnp.where(spot < width // 2, own, pltpu.roll(own, width - slot_lanes, own.ndim - 1))
        return jnp.where(spot >= width - slot_lanes, edges, value)

    center = merged[1 : 1 + groups]
    for f in range(4):
        block = ext[f, HALO : HALO + rows].reshape(groups, HALO, levels, width)
        for i in range(HALO):
            value = stitch(block[:, i], center, HALO * f + i)
            for g in range(groups):
                seam[f, HALO + HALO * g + i] = value[g]
    for half in range(2):
        piece = merged[half * (1 + groups)]
        for slot in range(slots):
            r = HALO + slots * half + slot
            seam[4, r] = stitch(ext[4, r], piece, slot)

    run_steps(seam, seam_work, rows, 8, "inner")

    outs = (temp_out, salt_out, east_out, north_out)

    def finish(some):
        for f, out in enumerate(outs):
            for r in some:
                edge = seam_work[5 + f, HALO + r]
                spot = lane_iota(edge.shape)
                value = main_work[5 + f, HALO + r]
                value = jnp.where(spot < HALO, edge, value)
                value = jnp.where(spot >= width - HALO, pltpu.roll(edge, slot_lanes, 1), value)
                out[pl.ds(r, levels, stride=rows), :] = value

    finish(range(HALO, rows - HALO))

    row_south.wait_recv()

    @pl.when(has_south)
    def _():
        pltpu.make_async_remote_copy(
            src_ref=ext.at[:, pl.ds(rows, HALO)],
            dst_ref=ext.at[:, pl.ds(0, HALO)],
            send_sem=row_send.at[0],
            recv_sem=row_recv.at[0],
            device_id=north_id,
            device_id_type=MESH,
        ).wait_recv()

    @pl.when(at_top)
    def _():
        for f in range(FIELDS):
            turned = swap_lanes(ext[f, north_base : north_base + HALO], width - 1)
            if f in (2, 3):
                turned = -turned
            for i in range(HALO):
                ext[f, north_base + i] = turned[HALO - 1 - i]

    run_steps(ext, main_work, rows, 8, "outer")

    corner_south.wait_recv()

    @pl.when(has_south)
    def _():
        pltpu.make_async_remote_copy(
            src_ref=merged.at[pl.ds(groups, 2)],
            dst_ref=corner.at[0],
            send_sem=corner_send.at[0],
            recv_sem=corner_recv.at[0],
            device_id=north_id,
            device_id_type=MESH,
        ).wait_recv()

    @pl.when(at_top)
    def _():
        fields = swap_lanes(corner[1, 0], slot_lanes * HALO - 1)
        fields = jnp.where(lane_iota(fields.shape) >= width // 2, -fields, fields)
        sea = swap_lanes(corner[1, 1], width - 1)
        corner[1, 0] = sea
        corner[1, 1] = fields

    for side in range(2):
        fields, sea = corner[side, side], corner[side, 1 - side]
        base = side * north_base
        for i in range(HALO):
            for f in range(4):
                seam[f, base + i] = stitch(ext[f, base + i], fields, HALO * f + i)
            slot = i if side else slots - HALO + i
            seam[4, base + i] = stitch(ext[4, base + i], sea, slot)

    run_steps(seam, seam_work, rows, 8, "outer")
    finish([*range(HALO), *range(rows - HALO, rows)])

    row_north.wait_send()
    to_left.wait_send()
    to_right.wait_send()
    corner_north.wait_send()

    @pl.when(has_south)
    def _():
        row_south.wait_send()
        corner_south.wait_send()


def write_out(*refs):
    count = (len(refs) - 1) // 2
    sems = refs[-1]
    copies = [
        pltpu.make_async_copy(refs[f], refs[count + f], sems.at[f]) for f in range(count)
    ]
    for copy in copies:
        copy.start()
    for copy in copies:
        copy.wait()


def shards(temp, salt, east, north, wet):
    levels, rows, columns = temp.shape
    flat = [x.reshape(levels * rows, columns) for x in (temp, salt, east, north, wet)]
    every = rows + 2 * HALO
    pieces = rows // HALO + 2
    plane = (levels, columns)
    vmem = lambda *lead: pltpu.VMEM(lead + plane, jnp.float32)
    flat = [pltpu.with_memory_space_constraint(x, pltpu.HBM) for x in flat]
    outs = pl.pallas_call(
        functools.partial(kernel, rows, levels),
        out_shape=[pltpu.VMEM((levels * rows, columns), jnp.float32)] * 4,
        in_specs=[pl.BlockSpec(memory_space=pltpu.HBM)] * 5,
        out_specs=[pl.BlockSpec(memory_space=pltpu.VMEM)] * 4,
        scratch_shapes=[
            pltpu.VMEM((4, levels * rows, columns), jnp.float32),
            pltpu.VMEM((levels * rows, columns), jnp.int32),
            vmem(FIELDS, every),
            vmem(FIELDS, every),
            vmem(10, every),
            vmem(10, every),
            vmem(pieces),
            vmem(pieces),
            vmem(pieces),
            vmem(pieces),
            vmem(2, 2),
            pltpu.SemaphoreType.DMA((FIELDS,)),
            pltpu.SemaphoreType.DMA((2,)),
            pltpu.SemaphoreType.DMA((2,)),
            pltpu.SemaphoreType.DMA((2,)),
            pltpu.SemaphoreType.DMA((2,)),
            pltpu.SemaphoreType.DMA((2,)),
            pltpu.SemaphoreType.DMA((2,)),
        ],
        compiler_params=pltpu.CompilerParams(
            collective_id=0, has_side_effects=True, vmem_limit_bytes=16 * 1024 * 1024
        ),
    )(*flat)
    outs = pl.pallas_call(
        write_out,
        out_shape=[jax.ShapeDtypeStruct((levels * rows, columns), jnp.float32)] * 4,
        in_specs=[pl.BlockSpec(memory_space=pltpu.VMEM)] * 4,
        out_specs=[pl.BlockSpec(memory_space=pltpu.HBM)] * 4,
        scratch_shapes=[pltpu.SemaphoreType.DMA((4,))],
        compiler_params=pltpu.CompilerParams(vmem_limit_bytes=2 * 1024 * 1024),
    )(*outs)
    return tuple(x.reshape(levels, rows, columns) for x in outs)


def solution(mesh):
    spec = P(None, "lat", "lon")
    return jax.shard_map(
        shards, mesh=mesh, in_specs=(spec,) * 5, out_specs=(spec,) * 4, check_vma=False
    )
```

```python
import functools

import jax
import jax.numpy as jnp
from jax import lax
from jax.experimental import pallas as pl
from jax.experimental.pallas import tpu as pltpu
from jax.sharding import PartitionSpec as P

STEPS = 2
TIME_STEP = 0.8
DIFFUSIVITY = 0.15
PRESSURE_GAIN = 0.12
LAYER_DEPTH = 0.5
HALO = 2 * STEPS
FIELDS = 5
MESH = pl.DeviceIdType.MESH


def lane_iota(shape):
    return lax.broadcasted_iota(jnp.int32, shape, len(shape) - 1)


def swap_lanes(x, bits):
    width = x.shape[-1]
    lane = lane_iota(x.shape)
    bit = 1
    while bit < width:
        if bits & bit:
            up = pltpu.roll(x, bit, x.ndim - 1)
            if 2 * bit == width:
                x = up
            else:
                x = jnp.where((lane & bit) != 0, up, pltpu.roll(x, width - bit, x.ndim - 1))
        bit *= 2
    return x


def blocks(first, count, size, body):
    start = first
    while start < first + count:
        body(start, min(size, first + count - start))
        start += size


def pressure_pass(temp, salt, load, first, count, size):
    def body(start, size):
        rows = pl.ds(start, size)
        total = (0.8 * LAYER_DEPTH) * salt[rows] - (0.2 * LAYER_DEPTH) * temp[rows]
        level = lax.broadcasted_iota(jnp.int32, total.shape, 1)
        shift = 1
        while shift < total.shape[1]:
            total = total + jnp.where(level >= shift, pltpu.roll(total, shift, 1), 0.0)
            shift *= 2
        load[rows] = total

    blocks(first, count, size, body)


def velocity_pass(load, wet, east, north, east_to, north_to, first, count, size):
    def body(start, size):
        rows = pl.ds(start, size)
        here = load[rows]
        width = here.shape[2]
        sea = wet[rows]
        grad_east = pltpu.roll(here, width - 1, 2) - pltpu.roll(here, 1, 2)
        grad_north = load[pl.ds(start + 1, size)] - load[pl.ds(start - 1, size)]
        east_to[rows] = (east[rows] - PRESSURE_GAIN * grad_east) * sea
        north_to[rows] = (north[rows] - PRESSURE_GAIN * grad_north) * sea

    blocks(first, count, size, body)


def tracer_pass(tracers, wet, east, north, tracers_to, first, count, size):
    def body(start, size):
        rows = pl.ds(start, size)
        around = pl.ds(start - 1, size + 2)
        sea = wet[around]
        inner = sea[1:-1]
        width = sea.shape[2]
        flow = east[rows]
        both = inner * pltpu.roll(inner, width - 1, 2)
        mean = 0.25 * (flow + pltpu.roll(flow, width - 1, 2))
        east_here, east_next = (mean + DIFFUSIVITY) * both, (mean - DIFFUSIVITY) * both
        rise = north[around]
        both = sea[:-1] * sea[1:]
        mean = 0.25 * (rise[:-1] + rise[1:])
        north_here, north_next = (mean + DIFFUSIVITY) * both, (mean - DIFFUSIVITY) * both
        scale = TIME_STEP * inner
        for tracer, tracer_to in zip(tracers, tracers_to):
            q = tracer[around]
            mid = q[1:-1]
            flux_east = east_here * mid + east_next * pltpu.roll(mid, width - 1, 2)
            flux_north = north_here * q[:-1] + north_next * q[1:]
            spread = flux_east - pltpu.roll(flux_east, 1, 2) + (flux_north[1:] - flux_north[:-1])
            tracer_to[rows] = mid - scale * spread

    blocks(first, count, size, body)


def run_steps(ext, work, rows, size, parts):
    every = rows + 2 * HALO
    wet = ext.at[4]
    held = [ext.at[f] for f in range(4)]
    for step in range(STEPS):
        load = work.at[9 * step]
        to = [work.at[1 + 4 * step + f] for f in range(4)]
        for reach in range(3):
            edge = 2 * step + reach
            whole = (edge, every - 2 * edge)
            inner = (edge + HALO, every - 2 * edge - 2 * HALO)
            outer = [(edge, HALO), (every - edge - HALO, HALO)]
            todo = {"inner": [inner], "outer": outer, "whole": [whole]}[parts]
            for first, count in todo:
                if reach == 0:
                    pressure_pass(held[0], held[1], load, first, count, size)
                elif reach == 1:
                    velocity_pass(load, wet, held[2], held[3], to[2], to[3], first, count, size)
                else:
                    tracer_pass(held[:2], wet, to[2], to[3], to[:2], first, count, size)
        held = to


def kernel(
    rows,
    levels,
    temp_hbm,
    salt_hbm,
    east_hbm,
    north_hbm,
    wet_hbm,
    temp_out,
    salt_out,
    east_out,
    north_out,
    staged,
    staged_wet,
    ext,
    seam,
    main_work,
    seam_work,
    packed,
    from_left,
    from_right,
    merged,
    corner,
    load_sem,
    row_send,
    row_recv,
    col_send,
    col_recv,
    corner_send,
    corner_recv,
):
    lon, lat = lax.axis_index("lon"), lax.axis_index("lat")
    lon_total, lat_total = lax.axis_size("lon"), lax.axis_size("lat")
    at_top = lat == lat_total - 1
    has_south = lat > 0
    left, right = lax.rem(lon + lon_total - 1, lon_total), lax.rem(lon + 1, lon_total)
    top = (lat // (lat_total - 1)) if lat_total > 1 else 1
    north_lon = lon + top * (lon_total - 1 - 2 * lon)
    north_lat = lat + 1 - top
    north_id = {"lon": north_lon, "lat": north_lat}
    south_id = {"lon": lon, "lat": lat - 1}
    left_id, right_id = {"lon": left, "lat": lat}, {"lon": right, "lat": lat}

    inputs = (temp_hbm, salt_hbm, east_hbm, north_hbm)
    loads = [pltpu.make_async_copy(h, staged.at[f], load_sem.at[f]) for f, h in enumerate(inputs)]
    loads.append(pltpu.make_async_copy(wet_hbm, staged_wet, load_sem.at[4]))
    for copy in loads:
        copy.start()

    barrier = pltpu.get_barrier_semaphore()
    for other in (left_id, right_id, north_id):
        pl.semaphore_signal(barrier, inc=1, device_id=other, device_id_type=MESH)

    @pl.when(has_south)
    def _():
        pl.semaphore_signal(barrier, inc=1, device_id=south_id, device_id_type=MESH)

    for f in range(FIELDS):
        loads[f].wait()
        for r in range(rows):
            if f < 4:
                value = staged[f, pl.ds(r, levels, stride=rows), :]
            else:
                value = staged_wet[pl.ds(r, levels, stride=rows), :].astype(jnp.float32)
            ext[f, HALO + r] = value

    width = ext.shape[-1]
    slot_lanes = 2 * HALO
    groups = rows // HALO
    gathered = jnp.zeros((groups, levels, width), jnp.float32)
    slot_of = lane_iota(gathered.shape) // slot_lanes
    for f in range(4):
        block = ext[f, HALO : HALO + rows].reshape(groups, HALO, levels, width)
        for i in range(HALO):
            slot = HALO * f + i
            turned = pltpu.roll(block[:, i], (HALO + slot_lanes * slot) % width, 2)
            gathered = jnp.where(slot_of == slot, turned, gathered)
    packed[1 : 1 + groups] = gathered
    slots = width // slot_lanes
    halves = jnp.zeros((2, levels, width), jnp.float32)
    slot_of = lane_iota(halves.shape) // slot_lanes
    block = ext[4, HALO : HALO + rows].reshape(2, slots, levels, width)
    for slot in range(slots):
        turned = pltpu.roll(block[:, slot], (HALO + slot_lanes * slot) % width, 2)
        halves = jnp.where(slot_of == slot, turned, halves)
    packed[0] = halves[0]
    packed[1 + groups] = halves[1]

    pl.semaphore_wait(barrier, 3 + jnp.minimum(lat, 1))

    north_base = HALO + rows
    row_north = pltpu.make_async_remote_copy(
        src_ref=ext.at[:, pl.ds(rows, HALO)],
        dst_ref=ext.at[:, pl.ds(top * north_base, HALO)],
        send_sem=row_send.at[0],
        recv_sem=row_recv.at[top],
        device_id=north_id,
        device_id_type=MESH,
    )
    row_south = pltpu.make_async_remote_copy(
        src_ref=ext.at[:, pl.ds(HALO, HALO)],
        dst_ref=ext.at[:, pl.ds(north_base, HALO)],
        send_sem=row_send.at[1],
        recv_sem=row_recv.at[1],
        device_id=south_id,
        device_id_type=MESH,
    )
    to_left = pltpu.make_async_remote_copy(
        src_ref=packed,
        dst_ref=from_right,
        send_sem=col_send.at[0],
        recv_sem=col_recv.at[1],
        device_id=left_id,
        device_id_type=MESH,
    )
    to_right = pltpu.make_async_remote_copy(
        src_ref=packed,
        dst_ref=from_left,
        send_sem=col_send.at[1],
        recv_sem=col_recv.at[0],
        device_id=right_id,
        device_id_type=MESH,
    )

    to_left.start()
    to_right.start()
    row_north.start()

    @pl.when(has_south)
    def _():
        row_south.start()

    @pl.when(lat == 0)
    def _():
        ext[:, 0:HALO] = jnp.zeros((FIELDS, HALO, levels, width), jnp.float32)
        corner[0] = jnp.zeros((2, levels, width), jnp.float32)

    run_steps(ext, main_work, rows, 16, "inner")

    to_left.wait_recv()
    to_right.wait_recv()
    before, after = from_left[...], from_right[...]
    lane = lane_iota(before.shape)
    merged[...] = jnp.where(
        (lane & HALO) != 0, pltpu.roll(before, HALO, 2), pltpu.roll(after, width - HALO, 2)
    )

    corner_north = pltpu.make_async_remote_copy(
        src_ref=merged.at[pl.ds(groups, 2)],
        dst_ref=corner.at[top],
        send_sem=corner_send.at[0],
        recv_sem=corner_recv.at[top],
        device_id=north_id,
        device_id_type=MESH,
    )
    corner_south = pltpu.make_async_remote_copy(
        src_ref=merged.at[pl.ds(0, 2)],
        dst_ref=corner.at[1],
        send_sem=corner_send.at[1],
        recv_sem=corner_recv.at[1],
        device_id=south_id,
        device_id_type=MESH,
    )
    corner_north.start()

    @pl.when(has_south)
    def _():
        corner_south.start()

    def stitch(own, piece, slot):
        spot = lane_iota(own.shape)
        edges = pltpu.roll(piece, (width - slot_lanes * (slot + 1)) % width, own.ndim - 1)
        value = jnp.where(spot < width // 2, own, pltpu.roll(own, width - slot_lanes, own.ndim - 1))
        return jnp.where(spot >= width - slot_lanes, edges, value)

    center = merged[1 : 1 + groups]
    for f in range(4):
        block = ext[f, HALO : HALO + rows].reshape(groups, HALO, levels, width)
        for i in range(HALO):
            value = stitch(block[:, i], center, HALO * f + i)
            for g in range(groups):
                seam[f, HALO + HALO * g + i] = value[g]
    for half in range(2):
        piece = merged[half * (1 + groups)]
        for slot in range(slots):
            r = HALO + slots * half + slot
            seam[4, r] = stitch(ext[4, r], piece, slot)

    run_steps(seam, seam_work, rows, 16, "inner")

    outs = (temp_out, salt_out, east_out, north_out)

    def finish(some):
        for f, out in enumerate(outs):
            for r in some:
                edge = seam_work[5 + f, HALO + r]
                spot = lane_iota(edge.shape)
                value = main_work[5 + f, HALO + r]
                value = jnp.where(spot < HALO, edge, value)
                value = jnp.where(spot >= width - HALO, pltpu.roll(edge, slot_lanes, 1), value)
                out[pl.ds(r, levels, stride=rows), :] = value

    finish(range(HALO, rows - HALO))

    row_south.wait_recv()

    @pl.when(has_south)
    def _():
        pltpu.make_async_remote_copy(
            src_ref=ext.at[:, pl.ds(rows, HALO)],
            dst_ref=ext.at[:, pl.ds(0, HALO)],
            send_sem=row_send.at[0],
            recv_sem=row_recv.at[0],
            device_id=north_id,
            device_id_type=MESH,
        ).wait_recv()

    @pl.when(at_top)
    def _():
        for f in range(FIELDS):
            turned = swap_lanes(ext[f, north_base : north_base + HALO], width - 1)
            if f in (2, 3):
                turned = -turned
            for i in range(HALO):
                ext[f, north_base + i] = turned[HALO - 1 - i]

    run_steps(ext, main_work, rows, 16, "outer")

    corner_south.wait_recv()

    @pl.when(has_south)
    def _():
        pltpu.make_async_remote_copy(
            src_ref=merged.at[pl.ds(groups, 2)],
            dst_ref=corner.at[0],
            send_sem=corner_send.at[0],
            recv_sem=corner_recv.at[0],
            device_id=north_id,
            device_id_type=MESH,
        ).wait_recv()

    @pl.when(at_top)
    def _():
        fields = swap_lanes(corner[1, 0], slot_lanes * HALO - 1)
        fields = jnp.where(lane_iota(fields.shape) >= width // 2, -fields, fields)
        sea = swap_lanes(corner[1, 1], width - 1)
        corner[1, 0] = sea
        corner[1, 1] = fields

    for side in range(2):
        fields, sea = corner[side, side], corner[side, 1 - side]
        base = side * north_base
        for i in range(HALO):
            for f in range(4):
                seam[f, base + i] = stitch(ext[f, base + i], fields, HALO * f + i)
            slot = i if side else slots - HALO + i
            seam[4, base + i] = stitch(ext[4, base + i], sea, slot)

    run_steps(seam, seam_work, rows, 16, "outer")
    finish([*range(HALO), *range(rows - HALO, rows)])

    row_north.wait_send()
    to_left.wait_send()
    to_right.wait_send()
    corner_north.wait_send()

    @pl.when(has_south)
    def _():
        row_south.wait_send()
        corner_south.wait_send()


def write_out(*refs):
    count = (len(refs) - 1) // 2
    sems = refs[-1]
    copies = [
        pltpu.make_async_copy(refs[f], refs[count + f], sems.at[f]) for f in range(count)
    ]
    for copy in copies:
        copy.start()
    for copy in copies:
        copy.wait()


def shards(temp, salt, east, north, wet):
    levels, rows, columns = temp.shape
    flat = [x.reshape(levels * rows, columns) for x in (temp, salt, east, north, wet)]
    every = rows + 2 * HALO
    pieces = rows // HALO + 2
    plane = (levels, columns)
    vmem = lambda *lead: pltpu.VMEM(lead + plane, jnp.float32)
    flat = [pltpu.with_memory_space_constraint(x, pltpu.HBM) for x in flat]
    outs = pl.pallas_call(
        functools.partial(kernel, rows, levels),
        out_shape=[pltpu.VMEM((levels * rows, columns), jnp.float32)] * 4,
        in_specs=[pl.BlockSpec(memory_space=pltpu.HBM)] * 5,
        out_specs=[pl.BlockSpec(memory_space=pltpu.VMEM)] * 4,
        scratch_shapes=[
            pltpu.VMEM((4, levels * rows, columns), jnp.float32),
            pltpu.VMEM((levels * rows, columns), jnp.int32),
            vmem(FIELDS, every),
            vmem(FIELDS, every),
            vmem(10, every),
            vmem(10, every),
            vmem(pieces),
            vmem(pieces),
            vmem(pieces),
            vmem(pieces),
            vmem(2, 2),
            pltpu.SemaphoreType.DMA((FIELDS,)),
            pltpu.SemaphoreType.DMA((2,)),
            pltpu.SemaphoreType.DMA((2,)),
            pltpu.SemaphoreType.DMA((2,)),
            pltpu.SemaphoreType.DMA((2,)),
            pltpu.SemaphoreType.DMA((2,)),
            pltpu.SemaphoreType.DMA((2,)),
        ],
        compiler_params=pltpu.CompilerParams(
            collective_id=0, has_side_effects=True, vmem_limit_bytes=16 * 1024 * 1024
        ),
    )(*flat)
    outs = pl.pallas_call(
        write_out,
        out_shape=[jax.ShapeDtypeStruct((levels * rows, columns), jnp.float32)] * 4,
        in_specs=[pl.BlockSpec(memory_space=pltpu.VMEM)] * 4,
        out_specs=[pl.BlockSpec(memory_space=pltpu.HBM)] * 4,
        scratch_shapes=[pltpu.SemaphoreType.DMA((4,))],
        compiler_params=pltpu.CompilerParams(vmem_limit_bytes=2 * 1024 * 1024),
    )(*outs)
    return tuple(x.reshape(levels, rows, columns) for x in outs)


def solution(mesh):
    spec = P(None, "lat", "lon")
    return jax.shard_map(
        shards, mesh=mesh, in_specs=(spec,) * 5, out_specs=(spec,) * 4, check_vma=False
    )
```
